32 devices in a mesh: expert: 4 (over y, core), hidden: 8 (over z, x).
Axes of the slice: x: 2, y: 2, z: 4, core: 2. Of those that a mesh axis runs over, the one named last changes fastest.
Arguments:
- tokens: bfloat16 [512, 3584], P('hidden'), may hold values from -6 to 6
- cotangent: bfloat16 [512, 3584], P('hidden'), may hold values from -6 to 6
- routes: int32 [512, 8], P('hidden'), may hold values from 0 to 63, all different within a row; in each aligned block of 64 rows (0 to 63, 64 to 127, ...) at most 20 rows name the same one
- route_weights: float32 [512, 8], P('hidden'), may hold values from 0.08 to 1
- gate_weight: bfloat16 [65536, 3584], P(('expert', 'hidden')), may hold values from -0.09375 to 0.09375
- up_weight: bfloat16 [65536, 3584], P(('expert', 'hidden')), may hold values from -0.09375 to 0.09375
- down_weight: bfloat16 [65536, 3584], P(('expert', 'hidden')), may hold values from -6 to 6
- cluster: int32 [64], replicated, may hold values from 0 to 23, as said below
- merged_slot: int32 [24], replicated, may hold values from 0 to 23, each once
Outputs:
- merged_down: bfloat16 [24, 1, 1024, 3584], P('expert', None, 'hidden')
The draws below stay inside these ranges and needn't reach their ends.
Inputs may be any that keep to these rules, and one draw needn't show every extreme that they name: `routes`: each row names 8 different experts. Within the rows of one shard of 64 tokens no expert is named by more than 20 rows, a bound that some block reaches. Every one of the 24 clusters has 1 to 6 member experts, and some cluster has exactly 6. `merged_slot`: each slot holds exactly one cluster.
All inputs are finite; a program needn't handle non-finite values.
Results may differ from the reference program's by a relative error of at most 0.014.
Values may be sent and summed in bfloat16 or wider, within the bound.
A program may use at most 192 MiB of HBM per device.

```python
import math
import jax
import jax.numpy as jnp
import numpy as np
from jax import lax

D = 3584
F = 1024
EXPERTS = 64
MERGED = 24
TOP = 8
TOK_DEV = 64
TOKENS = 512
CAP = 20
SLICE_ROWS = 1024
SLICE_COUNT = 1
N_EXPERT = 4
N_HIDDEN = 8


def draw_cluster(key, part):
    key_big, key_grow, key_order = jax.random.split(jax.random.fold_in(key, 11), 3)
    labels = jnp.arange(MERGED, dtype=jnp.int32)
    biggest = jax.random.randint(key_big, (), 0, MERGED, dtype=jnp.int32)
    counts = jnp.ones((MERGED,), jnp.int32) + 5 * (labels == biggest).astype(jnp.int32)
    grow_keys = jax.random.split(key_grow, EXPERTS - MERGED - 5)

    def grow(counts, subkey):
        scores = jax.random.randint(subkey, (MERGED,), 0, 1 << 20, dtype=jnp.int32) * MERGED + labels
        scores = jnp.where(counts < 6, scores, -1)
        chosen = jnp.argmax(scores).astype(jnp.int32)
        return (counts + (labels == chosen).astype(jnp.int32), None)
    counts, _ = lax.scan(grow, counts, grow_keys)
    bounds = jnp.cumsum(counts)
    positions = jnp.arange(EXPERTS, dtype=jnp.int32)
    cluster_at = jnp.sum((positions[:, None] >= bounds[None, :]).astype(jnp.int32), axis=1)
    shuffle = jax.random.permutation(key_order, EXPERTS).astype(jnp.int32)
    inverse = jnp.argsort(shuffle, stable=True)
    return cluster_at[inverse].astype(jnp.int32)


def token_scales(key):
    lowest = math.log(0.1)
    highest = math.log(0.8)
    return jnp.exp(jax.random.uniform(jax.random.fold_in(key, 21), (TOKENS,), jnp.float32, lowest, highest))


def draw_route_weights(key, part):
    scales = token_scales(key)
    spread_key = jax.random.fold_in(key, 22)
    spread_part = jnp.exp(jax.random.uniform(spread_key, (TOKENS, TOP), jnp.float32, math.log(0.8), math.log(1.25)))
    return (scales[:, None] * spread_part).astype(jnp.float32)


def draw_cotangent(key, part):
    scales = token_scales(key)
    blocks = 16
    hot_block = jax.random.randint(jax.random.fold_in(key, 23), (TOKENS,), 0, blocks, dtype=jnp.int32)
    cold_gain = jnp.exp(jax.random.uniform(jax.random.fold_in(key, 24), (TOKENS, blocks), jnp.float32, -2.5, -0.5))
    block_ids = jnp.arange(blocks, dtype=jnp.int32)
    base_key = jax.random.fold_in(key, 25)
    hot_gain = 2.5
    base_values = jax.random.normal(base_key, (TOKENS, D), jnp.float32)
    block_gain = jnp.where(block_ids[None, :] == hot_block[:, None], hot_gain, cold_gain)
    column_gain = jnp.repeat(block_gain, D // blocks, axis=1)
    values = base_values * column_gain * (0.2 / scales)[:, None]
    return jnp.clip(values, -6.0, 6.0).astype(jnp.bfloat16)


def block_levels(stream_key, extent, cuts, smallest, top_value):
    loudness, own = 1.0, jax.random.fold_in(stream_key, 6)
    for axis_at, parts in cuts:
        heights = jnp.exp(jax.random.uniform(jax.random.fold_in(own, axis_at), (parts,), jnp.float32, smallest / len(cuts), top_value / len(cuts)))
        loudness = loudness * jnp.repeat(heights, extent[axis_at] // parts).reshape([-1 if axis == axis_at else 1 for axis in range(len(extent))])
    return loudness


def shared_out(rng, own, number, rows, amount, top, bound, skew):
    ranking = jax.random.permutation(rng, amount)
    crowded, common = load_shares(amount, rows * top, bound, skew, True), load_shares(amount, rows * top, bound, skew, False)
    places = jnp.arange(amount)

    def named(lengths, turn):
        used = int((lengths > 0).sum())
        fixed = max(1, used // 4)
        moved = fixed + (places - fixed + turn * (used - fixed)) % max(1, amount - fixed)
        return jnp.zeros((amount,), jnp.int32).at[ranking[jnp.where(places < fixed, places, moved)]].set(jnp.asarray(lengths, jnp.int32))

    lengths = jnp.where(number % 4 == 0, named(crowded, number // 4), named(common, number - number // 4 - 1))
    mixed = jax.random.permutation(jax.random.fold_in(own, 3), amount)
    giver, taker = mixed[0:amount // 2 * 2:2], mixed[1:amount // 2 * 2:2]
    margin = jnp.minimum(lengths[giver] - 1, bound - lengths[taker]) // 2
    margin = jnp.where((giver == ranking[0]) | (taker == ranking[0]) | (lengths[taker] == 0), 0, jnp.maximum(margin, 0))
    moved = jax.random.randint(jax.random.fold_in(own, 4), (amount // 2,), 0, 1 << 20) % (margin + 1)
    lengths = lengths.at[giver].add(-moved).at[taker].add(moved)
    items = jnp.searchsorted(jnp.cumsum(lengths), jnp.arange(rows * top), side="right").astype(jnp.int32)
    grid = items.reshape(top, rows).T
    grid = grid[jax.random.permutation(jax.random.fold_in(own, 1), rows)]
    turn = jax.random.randint(jax.random.fold_in(own, 2), (rows, 1), 0, top)
    return jnp.take_along_axis(grid, (jnp.arange(top)[None, :] + turn) % top, axis=1)


def load_shares(number_of, total, most, lean, full):
    weights = [(1 << 20) // math.isqrt(standing ** lean) + 1 for standing in range(1, number_of + 1)]
    largest = most if full else min(most, max(-(-total // number_of), total * weights[0] // sum(weights)))
    least = 1 if total - largest >= number_of - 1 else 0
    given, spare = [largest] + [least] * (number_of - 1), total - largest - least * (number_of - 1)
    while spare > 0:
        movable = [i for i in range(1, number_of) if given[i] < largest] or [i for i in range(1, number_of) if given[i] < most]
        mass, left = sum([weights[i] for i in movable]), spare
        for i in movable:
            more = min(most - given[i], max(1, left * weights[i] // mass), spare)
            given[i] = given[i] + more
            spare = spare - more
    return np.array(given)


def bell_draw(rng, extent, width, bound, shards=(), held_as=jnp.bfloat16):
    level = block_levels(rng, extent, shards, -0.22, 0.18) if shards else 1.0
    result = jax.random.normal(rng, extent, jnp.float32) * width * level
    return jnp.minimum(jnp.maximum(result, -bound), bound).astype(held_as)


def setup_inputs(seed: int = 0) -> dict:
    arg_keys = jax.random.split(jax.random.key(seed), 10)
    tokens = bell_draw(arg_keys[0], (TOKENS, D), 1.0, 6.0, ((0, 8),))
    cotangent = draw_cotangent(jax.random.fold_in(arg_keys[9], 71), 0)
    routes_keys = jax.random.split(jax.random.fold_in(arg_keys[2], 1), TOKENS // TOK_DEV)
    routes_turns = jax.random.permutation(jax.random.fold_in(arg_keys[2], 3), TOKENS // TOK_DEV)
    routes = jax.vmap(lambda own, number: shared_out(jax.random.fold_in(arg_keys[2], 2), own, number, TOK_DEV, EXPERTS, TOP, CAP, 3))(routes_keys, routes_turns).reshape((TOKENS, TOP))
    route_weights = draw_route_weights(jax.random.fold_in(arg_keys[9], 71), 0)
    gate_weight = bell_draw(arg_keys[4], (EXPERTS * F, D), D ** -0.5, 0.09375, ((0, 32),))
    up_weight = bell_draw(arg_keys[5], (EXPERTS * F, D), D ** -0.5, 0.09375, ((0, 32),))
    down_weight = bell_draw(arg_keys[6], (EXPERTS * F, D), 1.0, 6.0, ((0, 32),))
    cluster = draw_cluster(jax.random.fold_in(arg_keys[9], 71), 0)
    merged_slot = jax.random.permutation(arg_keys[8], MERGED).astype(jnp.int32)
    return dict(tokens=tokens, cotangent=cotangent, routes=routes, route_weights=route_weights, gate_weight=gate_weight, up_weight=up_weight, down_weight=down_weight, cluster=cluster, merged_slot=merged_slot)


PRIOR = 0.1


def rounded(values):
    narrow = values.astype(jnp.bfloat16)
    narrow = lax.optimization_barrier(narrow)
    return narrow.astype(jnp.float32)


def reference(tokens, cotangent, routes, route_weights, gate_weight, up_weight, down_weight, cluster, merged_slot):
    group_size = EXPERTS // N_EXPERT
    token_wide = tokens.astype(jnp.float32).reshape(N_HIDDEN, TOK_DEV, D)
    cot_wide = cotangent.astype(jnp.float32).reshape(N_HIDDEN, TOK_DEV, D)
    route_blocks = routes.reshape(N_HIDDEN, TOK_DEV, TOP)
    weight_blocks = route_weights.reshape(N_HIDDEN, TOK_DEV, TOP)
    merged_ids = jnp.arange(MERGED, dtype=jnp.int32)
    slot_table = jnp.sum(jnp.where(cluster[:, None] == merged_ids[None, :], merged_slot[None, :], 0), axis=1)
    places_all = jnp.arange(CAP, dtype=jnp.int32)
    expert_ids = jnp.arange(EXPERTS, dtype=jnp.int32)

    def expert_terms(expert):
        matches = route_blocks == expert
        marked = jnp.any(matches, axis=2).astype(jnp.int32)
        places = jnp.cumsum(marked, axis=1) - marked
        slot_weight = jnp.sum(jnp.where(matches, weight_blocks, 0.0), axis=2)
        chosen = (marked[:, None, :] == 1) & (places[:, None, :] == places_all[None, :, None])
        picker = jnp.where(chosen, 1.0, 0.0).astype(jnp.float32)
        token_rows = jnp.einsum("hct,htd->hcd", picker, token_wide).astype(jnp.bfloat16).reshape(N_HIDDEN * CAP, D)
        cot_rows = jnp.einsum("hct,htd->hcd", picker, cot_wide)
        scales = jnp.sum(picker * slot_weight[:, None, :], axis=2)
        grad_rows = (scales[:, :, None] * cot_rows).astype(jnp.bfloat16).reshape(N_HIDDEN * CAP, D)
        start = (expert * F).astype(jnp.int32)
        gate_rows = lax.dynamic_slice_in_dim(gate_weight, start, F, 0)
        up_rows = lax.dynamic_slice_in_dim(up_weight, start, F, 0)
        down_rows = lax.dynamic_slice_in_dim(down_weight, start, F, 0)
        dims = (((1,), (1,)), ((), ()))
        gate_value = lax.dot_general(token_rows, gate_rows, dims, preferred_element_type=jnp.float32)
        up_value = lax.dot_general(token_rows, up_rows, dims, preferred_element_type=jnp.float32)
        hidden_act = jax.nn.silu(gate_value) * up_value
        hidden_sq = (hidden_act * hidden_act).astype(jnp.bfloat16)
        grad_wide = grad_rows.astype(jnp.float32)
        grad_sq = (grad_wide * grad_wide).astype(jnp.bfloat16)
        fisher = jnp.dot(hidden_sq.T, grad_sq, preferred_element_type=jnp.float32)
        weighting = fisher + PRIOR
        numer = (weighting * down_rows.astype(jnp.float32)).astype(jnp.bfloat16)
        denom = weighting.astype(jnp.bfloat16)
        return numer, denom

    def group_step(carry, group_id):
        members = group_id * group_size + jnp.arange(group_size, dtype=jnp.int32)
        numer, denom = lax.map(expert_terms, members)
        member_slots = jnp.sum(jnp.where(members[:, None] == expert_ids[None, :], slot_table[None, :], 0), axis=1)
        mixer = jnp.where(member_slots[None, :] == merged_ids[:, None], 1.0, 0.0).astype(jnp.float32)
        numer_part = jnp.einsum("me,efd->mfd", mixer, numer.astype(jnp.float32))
        denom_part = jnp.einsum("me,efd->mfd", mixer, denom.astype(jnp.float32))
        return (carry[0] + rounded(numer_part), carry[1] + rounded(denom_part)), None

    zeros = jnp.zeros((MERGED, F, D), jnp.float32)
    totals, _ = lax.scan(group_step, (zeros, zeros), jnp.arange(N_EXPERT, dtype=jnp.int32))
    merged = (totals[0] / totals[1]).astype(jnp.bfloat16)
    return merged.reshape(MERGED, SLICE_COUNT, SLICE_ROWS, D)
```

```python
import jax
import jax.numpy as jnp
from jax import lax
from jax.experimental import pallas as pl
from jax.experimental.pallas import tpu as pltpu
from jax.sharding import PartitionSpec as P

F = 1024
EXPERTS = 64
MERGED = 24

PRIOR = 0.1


def slot_lookup(cluster, merged_slot):
    merged_ids = jnp.arange(MERGED, dtype=jnp.int32)
    return jnp.sum(
        jnp.where(cluster[:, None] == merged_ids[None, :], merged_slot[None, :], 0), axis=1
    )


def chunk_bounds(width):
    if width % (7 * 128):
        return [(0, width)]
    unit = width // 7
    cuts = [0, 2 * unit, 4 * unit, 6 * unit, 7 * unit]
    return list(zip(cuts[:-1], cuts[1:]))


def fold_kernel(slots_ref, act_ref, cot_ref, down_ref, out_ref, total):
    total[...] = jnp.zeros_like(total)
    for unit in range(act_ref.shape[0]):
        fisher = jnp.dot(act_ref[unit], cot_ref[...], preferred_element_type=jnp.float32)
        numer = (fisher + PRIOR) * down_ref[unit].astype(jnp.float32)
        slot = slots_ref[unit]
        total[slot] = total[slot] + numer
    out_ref[...] = total[...].astype(out_ref.dtype)


def fold(unit_slots, act, cot_sq, down, slot_count):
    units, piece, tok_count = act.shape
    width = down.shape[-1]
    block = 512 if width % 512 == 0 else (256 if width % 256 == 0 else 128)
    return pl.pallas_call(
        fold_kernel,
        grid_spec=pltpu.PrefetchScalarGridSpec(
            num_scalar_prefetch=1,
            grid=(width // block,),
            in_specs=[
                pl.BlockSpec((units, piece, tok_count), lambda i, s: (0, 0, 0)),
                pl.BlockSpec((tok_count, block), lambda i, s: (0, i)),
                pl.BlockSpec((units, piece, block), lambda i, s: (0, 0, i)),
            ],
            out_specs=pl.BlockSpec((slot_count, piece, block), lambda i, s: (0, 0, i)),
            scratch_shapes=[pltpu.VMEM((slot_count, piece, block), jnp.float32)],
        ),
        out_shape=jax.ShapeDtypeStruct((slot_count, piece, width), jnp.bfloat16),
        compiler_params=pltpu.CompilerParams(vmem_limit_bytes=40 * 1024 * 1024),
        cost_estimate=pl.CostEstimate(
            flops=2 * units * piece * tok_count * width,
            bytes_accessed=2 * (units + slot_count) * piece * width,
            transcendentals=0,
        ),
    )(unit_slots, act, cot_sq, down)


def per_device(
    tokens,
    cotangent,
    routes,
    route_weights,
    gate_weight,
    up_weight,
    down_weight,
    cluster,
    merged_slot,
):
    hidden_count = lax.axis_size("hidden")
    expert_count = lax.axis_size("expert")
    expert_index = lax.axis_index("expert")
    hidden_index = lax.axis_index("hidden")
    rows_dev, width = gate_weight.shape
    local_count = max(1, rows_dev // F)
    slice_rows = min(rows_dev, F)
    copies = F // slice_rows
    group_size = EXPERTS // expert_count
    piece = slice_rows // hidden_count
    first_expert = expert_index * group_size
    units = hidden_count * local_count
    slot_count = MERGED * copies
    own_slots = MERGED // expert_count
    top = routes.shape[1]

    down_view = down_weight.reshape(local_count, hidden_count, piece, width)
    bounds = chunk_bounds(width)

    def exchange(rows):
        return lax.all_to_all(rows, "hidden", split_axis=0, concat_axis=0, tiled=True)

    def down_send(lo, hi):
        return jnp.swapaxes(down_view[..., lo:hi], 0, 1)

    choice = jnp.concatenate([routes.astype(jnp.float32), route_weights], axis=1)
    tokens_all = lax.all_gather(tokens, "hidden", axis=0, tiled=True)
    choice_all = lax.all_gather(choice, "hidden", axis=0, tiled=True)
    cot_wide = cotangent.astype(jnp.float32)
    cot_sq = lax.all_gather(
        (cot_wide * cot_wide).astype(jnp.bfloat16), "hidden", axis=0, tiled=True
    )
    tok_count = tokens_all.shape[0]

    start_own = hidden_index * rows_dev + jnp.arange(local_count, dtype=jnp.int32) * slice_rows
    own_expert = (first_expert + start_own // F).astype(jnp.float32)
    named = choice_all[None, :, :top] == own_expert[:, None, None]
    weight_own = jnp.sum(jnp.where(named, choice_all[None, :, top:], 0.0), axis=2)
    dims = (((1,), (1,)), ((), ()))
    gate_value = lax.dot_general(
        gate_weight, tokens_all, dims, preferred_element_type=jnp.float32
    )
    up_value = lax.dot_general(up_weight, tokens_all, dims, preferred_element_type=jnp.float32)
    scaled = (jax.nn.silu(gate_value) * up_value).reshape(local_count, slice_rows, tok_count)
    scaled = scaled * weight_own[:, None, :]
    act = (scaled * scaled).astype(jnp.bfloat16)
    act = jnp.swapaxes(act.reshape(local_count, hidden_count, piece, tok_count), 0, 1)

    first = exchange(down_send(*bounds[0]))
    act, first = lax.optimization_barrier((act, first))
    act_units = exchange(act).reshape(units, piece, tok_count)

    sources = jnp.arange(hidden_count, dtype=jnp.int32)[:, None]
    local_ids = jnp.arange(local_count, dtype=jnp.int32)[None, :]
    start_row = (sources * rows_dev + local_ids * slice_rows).reshape(units)
    slot_table = slot_lookup(cluster, merged_slot)
    expert_ids = jnp.arange(EXPERTS, dtype=jnp.int32)
    unit_expert = first_expert + start_row // F
    unit_slot = jnp.sum(
        jnp.where(unit_expert[:, None] == expert_ids[None, :], slot_table[None, :], 0), axis=1
    )
    unit_slots = unit_slot * copies + start_row % F // slice_rows
    mixer = (
        unit_slots[None, :] == jnp.arange(slot_count, dtype=jnp.int32)[:, None]
    ).astype(jnp.bfloat16)

    act_part = jnp.einsum("su,uqt->sqt", mixer, act_units, preferred_element_type=jnp.float32)
    act_total = lax.psum_scatter(
        act_part.astype(jnp.bfloat16).reshape(MERGED, copies, piece, tok_count),
        "expert",
        scatter_dimension=0,
        tiled=True,
    )
    own_ids = expert_index * own_slots + jnp.arange(own_slots, dtype=jnp.int32)
    member_count = jnp.sum((slot_table[None, :] == own_ids[:, None]).astype(jnp.float32), axis=1)
    prior = PRIOR * member_count[:, None, None, None]

    merged = []
    numer_part, events = None, []
    for lo, hi in bounds:
        if numer_part is None:
            rows = first
        else:
            held = (down_send(lo, hi), numer_part, events[-2:-1])
            send, numer_part, _ = lax.optimization_barrier(held)
            rows = exchange(send)
        numer_part = fold(
            unit_slots,
            act_units,
            cot_sq[:, lo:hi],
            rows.reshape(units, piece, hi - lo),
            slot_count,
        )
        ready, _ = lax.optimization_barrier((numer_part, events[-1:]))
        numer_total = lax.psum_scatter(
            ready.reshape(MERGED, copies, piece, hi - lo),
            "expert",
            scatter_dimension=0,
            tiled=True,
        )
        events.append((numer_total, act_total))
        denom = jnp.einsum(
            "scqt,td->scqd", act_total, cot_sq[:, lo:hi], preferred_element_type=jnp.float32
        )
        merged.append((numer_total.astype(jnp.float32) / (denom + prior)).astype(jnp.bfloat16))
    return jnp.concatenate(merged, axis=3)


def solution(mesh):
    return jax.shard_map(
        per_device,
        mesh=mesh,
        in_specs=(
            P("hidden", None),
            P("hidden", None),
            P("hidden", None),
            P("hidden", None),
            P(("expert", "hidden"), None),
            P(("expert", "hidden"), None),
            P(("expert", "hidden"), None),
            P(),
            P(),
        ),
        out_specs=P("expert", None, "hidden", None),
        check_vma=False,
    )
```
